256 devices in a mesh: ta: 2 (over x_lo), gx: 128 (over y, x_hi, z, core).
Axes of the slice: x: 4 (x_hi: 2, x_lo: 2; x = x_hi * 2 + x_lo), y: 4, z: 8, core: 2. Of those that a mesh axis runs over, the one named last changes fastest.
Arguments:
- voltages: bfloat16 [1024, 1048576], P('gx', 'ta'), may hold values from -8 to 7, as said below
Outputs:
- visibility: float32 [2, 128, 1024, 1024], P(None, 'gx', 'ta')
The draws below stay inside these ranges and needn't reach their ends.
Inputs may be any that keep to these rules, and one draw needn't show every extreme that they name: `voltages`: integer values: 4-bit quantized samples, a noise part plus a sky signal common to the inputs with integer gains.
All inputs are finite; a program needn't handle non-finite values.
Results may differ from the reference program's by a relative error of at most 0.00075.
Values may be sent and summed in bfloat16 or wider, within the bound.
No kernel may reach another device: no remote copies, remote signals or barrier semaphores. Data moves between devices by JAX's collectives and lax.ppermute only.
A program may use at most 64 MiB of HBM per device.

```python
import jax
import jax.numpy as jnp
from jax import lax

NI = 1024
FRAME = 2048
TAPS = 4
NCH = 128
SPECTRA = 512
SAMPLES = 1048576


def draw_voltages(key, part):
    key = jax.random.fold_in(key, 11)
    noise_key = jax.random.fold_in(key, 1)
    source_key = jax.random.fold_in(key, 2)
    gain_key = jax.random.fold_in(key, 3)
    noise_part = jax.random.randint(noise_key, (NI, SAMPLES), -6, 7)
    source = jax.random.randint(source_key, (1, SAMPLES), -3, 4)
    input_gain = jax.random.randint(gain_key, (NI, 1), 0, 3)
    summed = jnp.clip(noise_part + input_gain * source, -8, 7)
    return summed.astype(jnp.float32).astype(jnp.bfloat16)


def setup_inputs(seed: int = 0) -> dict:
    keys = jax.random.split(jax.random.key(seed), 2)
    return {
        "voltages": draw_voltages(jax.random.fold_in(keys[1], 71), 0),
    }


def pfb_window():
    length = TAPS * FRAME
    points = jnp.arange(length, dtype=jnp.float32)
    shaped = jnp.sinc((points - length / 2 + 0.5) / FRAME) * (0.54 - 0.46 * jnp.cos(2.0 * jnp.pi * points / (length - 1)))
    return shaped.reshape(TAPS, FRAME)


def dft_table(count):
    channel = jnp.arange(count, dtype=jnp.int32)[:, None]
    sample = jnp.arange(FRAME, dtype=jnp.int32)[None, :]
    phase = ((channel * sample) % FRAME).astype(jnp.float32) * (2.0 * jnp.pi / FRAME)
    return jnp.concatenate([jnp.cos(phase), -jnp.sin(phase)], 0)


def filter_frames(padded, span):
    window = pfb_window()
    filtered = window[0][None, None, :] * padded[:, 0:span, :].astype(jnp.float32)
    for tap_index in range(1, TAPS):
        filtered = filtered + window[tap_index][None, None, :] * padded[:, tap_index:tap_index + span, :].astype(jnp.float32)
    return filtered


def reference(voltages):
    group_size = 8
    grouped = voltages.reshape(NI // group_size, group_size, SPECTRA, FRAME)
    dft_rows = dft_table(NCH)

    def one_group(frames):
        padded = jnp.concatenate([jnp.zeros((group_size, TAPS - 1, FRAME), frames.dtype), frames], 1)
        filtered = filter_frames(padded, SPECTRA)
        result = jnp.einsum('isn,cn->cis', filtered, dft_rows, precision=lax.Precision.HIGHEST)
        return result.astype(jnp.bfloat16)

    stacked = lax.map(one_group, grouped)
    spectra = jnp.transpose(stacked, (1, 0, 2, 3)).reshape(2, NCH, NI, SPECTRA)
    norm_scale = 1.0 / (16.0 * FRAME * SPECTRA)

    def one_channel(index):
        chosen = lax.dynamic_index_in_dim(spectra, index, 1, keepdims=False)
        real_part = chosen[0]
        imag_part = chosen[1]
        vis_real = jnp.dot(real_part, real_part.T, preferred_element_type=jnp.float32) + jnp.dot(imag_part, imag_part.T, preferred_element_type=jnp.float32)
        vis_imag = jnp.dot(imag_part, real_part.T, preferred_element_type=jnp.float32) - jnp.dot(real_part, imag_part.T, preferred_element_type=jnp.float32)
        return jnp.stack([vis_real, vis_imag]) * norm_scale

    channels = lax.map(one_channel, jnp.arange(NCH, dtype=jnp.int32))
    return jnp.transpose(channels, (1, 0, 2, 3))
```

```python
import functools

import jax
import jax.numpy as jnp
import ml_dtypes
import numpy as np
from jax import lax
from jax.experimental import pallas as pl
from jax.experimental.pallas import tpu as pltpu
from jax.sharding import PartitionSpec as P

FRAME = 2048
TAPS = 4
BLOCK = 128
HALO = 4
VMEM = 56 * 1024 * 1024


def folded_table(count):
    length = TAPS * FRAME
    points = np.arange(length, dtype=np.float64)
    window = np.sinc((points - length / 2 + 0.5) / FRAME) * (
        0.54 - 0.46 * np.cos(2.0 * np.pi * points / (length - 1))
    )
    window = window.reshape(TAPS, FRAME)
    phase = (np.arange(FRAME)[:, None] * np.arange(count)[None, :] % FRAME) * (
        2.0 * np.pi / FRAME
    )
    dft = np.concatenate([np.cos(phase), -np.sin(phase)], 1)
    return (window[:, :, None] * dft[None]).astype(ml_dtypes.bfloat16)


def filterbank_kernel(frames, halo, table, out, rows, summed, turned):
    tap = pl.program_id(1)
    inputs = frames.shape[1]
    count = out.shape[0]
    span = BLOCK * inputs

    @pl.when(tap == 0)
    def _():
        rows[0 : HALO * inputs, :] = (
            halo[0].astype(jnp.float32).reshape(HALO * inputs, FRAME).astype(jnp.bfloat16)
        )

        def pack(step, carry):
            some = frames[pl.ds(step * 4, 4)].astype(jnp.float32)
            at = pl.multiple_of(HALO * inputs + step * 4 * inputs, 16)
            rows[pl.ds(at, 4 * inputs), :] = some.reshape(4 * inputs, FRAME).astype(jnp.bfloat16)
            return carry

        lax.fori_loop(0, BLOCK // 4, pack, 0)

    product = jnp.dot(rows[...], table[0], preferred_element_type=jnp.float32)

    for k in range(TAPS):

        @pl.when(tap == k)
        def _():
            start = (k + HALO - TAPS + 1) * inputs
            term = product[start : start + span]
            for part in range(2):
                half = term[:, part * count : (part + 1) * count]
                if k == 0:
                    summed[part] = half
                else:
                    summed[part] += half

    @pl.when(tap == TAPS - 1)
    def _():
        for part in range(2):
            for i in range(inputs):
                one = summed[part, pl.ds(i, BLOCK, stride=inputs), :]
                turned[pl.ds(part * inputs + i, count, stride=2 * inputs), :] = one.T
        out[...] = turned[...].reshape(count, 2 * inputs, BLOCK).astype(jnp.bfloat16)


def filterbank(frames, halo, table):
    spectra, inputs, _ = frames.shape
    count = table.shape[2] // 2
    blocks = spectra // BLOCK
    return pl.pallas_call(
        filterbank_kernel,
        grid=(blocks, TAPS),
        in_specs=[
            pl.BlockSpec((BLOCK, inputs, FRAME), lambda b, k: (b, 0, 0)),
            pl.BlockSpec((1, HALO, inputs, FRAME), lambda b, k: (b, 0, 0, 0)),
            pl.BlockSpec((1, FRAME, 2 * count), lambda b, k: (k, 0, 0)),
        ],
        out_specs=pl.BlockSpec((count, 2 * inputs, BLOCK), lambda b, k: (0, 0, b)),
        out_shape=jax.ShapeDtypeStruct((count, 2 * inputs, spectra), jnp.bfloat16),
        scratch_shapes=[
            pltpu.VMEM(((HALO + BLOCK) * inputs, FRAME), jnp.bfloat16),
            pltpu.VMEM((2, BLOCK * inputs, count), jnp.float32),
            pltpu.VMEM((2 * inputs * count, BLOCK), jnp.float32),
        ],
        compiler_params=pltpu.CompilerParams(vmem_limit_bytes=VMEM),
    )(frames, halo, table)


def visibility_kernel(scale, row_tile, where, mine, other, out, left, right):
    step = pl.program_id(0)
    groups, both, span = mine.shape
    per = both // 2
    total = groups * per

    @pl.when(step == 0)
    def _():
        for t, source in enumerate((mine, other)):
            wide = source[...].astype(jnp.float32).reshape(groups, 2, per, span)
            real = wide[:, 0].reshape(total, span)
            imag = wide[:, 1].reshape(total, span)
            at, far = t * span, (2 + t) * span
            right[:, at : at + span] = real.astype(jnp.bfloat16)
            right[:, far : far + span] = imag.astype(jnp.bfloat16)
            left[:, at : at + span] = imag.astype(jnp.bfloat16)
            left[:, far : far + span] = (-real).astype(jnp.bfloat16)

    first = pl.multiple_of(where[0] + step * row_tile, row_tile)
    dims = (((1,), (1,)), ((), ()))
    out[0, 0] = (
        lax.dot_general(
            right[pl.ds(first, row_tile), :], right[...], dims, preferred_element_type=jnp.float32
        )
        * scale
    )
    out[1, 0] = (
        lax.dot_general(
            left[pl.ds(first, row_tile), :], right[...], dims, preferred_element_type=jnp.float32
        )
        * scale
    )


def visibilities(mine, other, first_row, n_rows, scale):
    groups, both, span = mine.shape
    total = groups * both // 2
    row_tile = 128
    whole = pl.BlockSpec((groups, both, span), lambda r, w: (0, 0, 0))
    return pl.pallas_call(
        functools.partial(visibility_kernel, scale, row_tile),
        grid_spec=pltpu.PrefetchScalarGridSpec(
            num_scalar_prefetch=1,
            grid=(n_rows // row_tile,),
            in_specs=[whole, whole],
            out_specs=pl.BlockSpec((2, 1, row_tile, total), lambda r, w: (0, 0, r, 0)),
            scratch_shapes=[
                pltpu.VMEM((total, 4 * span), jnp.bfloat16),
                pltpu.VMEM((total, 4 * span), jnp.bfloat16),
            ],
        ),
        out_shape=jax.ShapeDtypeStruct((2, 1, n_rows, total), jnp.float32),
        compiler_params=pltpu.CompilerParams(vmem_limit_bytes=VMEM),
    )(first_row, mine, other)


def local(voltages):
    inputs = voltages.shape[0]
    spectra = voltages.shape[1] // FRAME
    n_time = lax.axis_size("ta")
    n_chan = lax.axis_size("gx")
    table = jnp.asarray(folded_table(n_chan))
    frames = voltages.reshape(inputs, spectra, FRAME).transpose(1, 0, 2)
    last = voltages[:, (spectra - HALO) * FRAME :]
    earlier = lax.ppermute(last, "ta", [(i, i + 1) for i in range(n_time - 1)])
    inner = [voltages[:, (b * BLOCK - HALO) * FRAME : b * BLOCK * FRAME] for b in range(1, spectra // BLOCK)]
    halo = jnp.stack([h.reshape(inputs, HALO, FRAME).transpose(1, 0, 2) for h in [earlier, *inner]])
    spectrum = filterbank(frames, halo, table)
    turned = lax.all_to_all(spectrum, "gx", split_axis=0, concat_axis=0, tiled=True)
    other = lax.ppermute(turned, "ta", [(i, (i + 1) % n_time) for i in range(n_time)])
    n_inputs = inputs * n_chan
    n_rows = n_inputs // n_time
    first_row = (lax.axis_index("ta") * n_rows).astype(jnp.int32).reshape(1)
    scale = 1.0 / (16.0 * FRAME * spectra * n_time)
    return visibilities(turned, other, first_row, n_rows, scale)


def solution(mesh):
    in_specs = (P("gx", "ta"),)
    out_specs = P(None, "gx", "ta", None)
    return jax.shard_map(local, mesh=mesh, in_specs=in_specs, out_specs=out_specs, check_vma=False)
```

```python
import functools

import jax
import jax.numpy as jnp
import ml_dtypes
import numpy as np
from jax import lax
from jax.experimental import pallas as pl
from jax.experimental.pallas import tpu as pltpu
from jax.sharding import Mesh
from jax.sharding import PartitionSpec as P

FRAME = 2048
TAPS = 4
BLOCK = 128
HALO = 4
COLUMNS = 256
VMEM = 56 * 1024 * 1024
VMEM_VIS = 28 * 1024 * 1024
PLANE = ("y", "z", "core")
MIB = 1024 * 1024


def folded_table(order):
    length = TAPS * FRAME
    points = np.arange(length, dtype=np.float64)
    window = np.sinc((points - length / 2 + 0.5) / FRAME) * (
        0.54 - 0.46 * np.cos(2.0 * np.pi * points / (length - 1))
    )
    window = window.reshape(TAPS, FRAME)
    phase = (np.arange(FRAME)[:, None] * order[None, :] % FRAME) * (2.0 * np.pi / FRAME)
    dft = np.concatenate([np.cos(phase), -np.sin(phase)], 1)
    return (window[:, :, None] * dft[None]).astype(ml_dtypes.bfloat16)


def filterbank_kernel(frames, halo, table, out, rows, summed, turned):
    tap = pl.program_id(0)
    inputs = frames.shape[1]
    count = out.shape[0]
    span = BLOCK * inputs

    @pl.when(tap == 0)
    def _():
        rows[0 : HALO * inputs, :] = (
            halo[...].astype(jnp.float32).reshape(HALO * inputs, FRAME).astype(jnp.bfloat16)
        )

        def pack(step, carry):
            some = frames[pl.ds(step * 4, 4)].astype(jnp.float32)
            at = pl.multiple_of(HALO * inputs + step * 4 * inputs, 16)
            rows[pl.ds(at, 4 * inputs), :] = some.reshape(4 * inputs, FRAME).astype(jnp.bfloat16)
            return carry

        lax.fori_loop(0, BLOCK // 4, pack, 0)

    product = jnp.dot(rows[...], table[0], preferred_element_type=jnp.float32)

    for k in range(TAPS):

        @pl.when(tap == k)
        def _():
            start = (k + HALO - TAPS + 1) * inputs
            term = product[start : start + span]
            for part in range(2):
                half = term[:, part * count : (part + 1) * count]
                if k == 0:
                    summed[part] = half
                else:
                    summed[part] += half

    @pl.when(tap == TAPS - 1)
    def _():
        for part in range(2):
            for i in range(inputs):
                one = summed[part, pl.ds(i, BLOCK, stride=inputs), :]
                turned[pl.ds(part * inputs + i, count, stride=2 * inputs), :] = one.T
        out[...] = turned[...].reshape(count, 2 * inputs, BLOCK).astype(jnp.bfloat16)


def filterbank(frames, block, halo, halo_block, table):
    _, inputs, _ = frames.shape
    count = table.shape[2] // 2
    return pl.pallas_call(
        filterbank_kernel,
        grid=(TAPS,),
        in_specs=[
            pl.BlockSpec((BLOCK, inputs, FRAME), lambda k: (block, 0, 0)),
            pl.BlockSpec((HALO, inputs, FRAME), lambda k: (halo_block, 0, 0)),
            pl.BlockSpec((1, FRAME, 2 * count), lambda k: (k, 0, 0)),
        ],
        out_specs=pl.BlockSpec((count, 2 * inputs, BLOCK), lambda k: (0, 0, 0)),
        out_shape=jax.ShapeDtypeStruct((count, 2 * inputs, BLOCK), jnp.bfloat16),
        scratch_shapes=[
            pltpu.VMEM(((HALO + BLOCK) * inputs, FRAME), jnp.bfloat16),
            pltpu.VMEM((2, BLOCK * inputs, count), jnp.float32),
            pltpu.VMEM((2 * inputs * count, BLOCK), jnp.float32),
        ],
        compiler_params=pltpu.CompilerParams(vmem_limit_bytes=VMEM),
        cost_estimate=pl.CostEstimate(
            flops=2 * BLOCK * inputs * FRAME * TAPS * 2 * count,
            bytes_accessed=9 * MIB,
            transcendentals=0,
        ),
    )(frames, halo, table)


def visibility_kernel(scale, half, where, *refs):
    sources, (out, right, left) = refs[:-3], refs[-3:]
    step = pl.program_id(0)
    x_hi, first_row = where[0], where[1]
    groups, both, span = sources[0].shape
    per = both // 2
    rows = half * 2
    n_y = 4
    stripe = groups // n_y * per
    n_rows = left.shape[0] // 2
    depth = right.shape[1] // 2

    @pl.when(step == 0)
    def _():
        for at, source in enumerate(sources):
            segment, far_x = at // 2, at % 2
            from_x = (x_hi + far_x) % 2
            for y in range(n_y):
                some = source[y * (groups // n_y) : (y + 1) * (groups // n_y)]
                wide = some.astype(jnp.float32).reshape(groups // n_y, 2, per, span)
                row = pl.multiple_of((y * 2 + from_x) * stripe, stripe)
                for part in range(2):
                    column = part * depth + segment * span
                    right[pl.ds(row, stripe), column : column + span] = (
                        wide[:, part].reshape(stripe, span).astype(jnp.bfloat16)
                    )
        own = right[pl.ds(pl.multiple_of(first_row, n_rows), n_rows), :]
        left[0:n_rows, :] = own
        left[n_rows:, 0:depth] = own[:, depth:]
        left[n_rows:, depth:] = -own[:, 0:depth]

    at = pl.multiple_of(step * COLUMNS, COLUMNS)
    product = lax.dot_general(
        left[...],
        right[pl.ds(at, COLUMNS), :],
        (((1,), (1,)), ((), ())),
        preferred_element_type=jnp.float32,
    )
    out[0, 0] = product[0:n_rows] * scale
    out[1, 0] = product[n_rows:] * scale


def visibilities(sources, where, n_rows, scale):
    groups, both, span = sources[0].shape
    total = groups * both
    depth = span * len(sources) // 2
    whole = pl.BlockSpec((groups, both, span), lambda r, w: (0, 0, 0))
    return pl.pallas_call(
        functools.partial(visibility_kernel, scale, total // 2),
        grid_spec=pltpu.PrefetchScalarGridSpec(
            num_scalar_prefetch=1,
            grid=(total // COLUMNS,),
            in_specs=[whole] * len(sources),
            out_specs=pl.BlockSpec((2, 1, n_rows, COLUMNS), lambda r, w: (0, 0, 0, r)),
            scratch_shapes=[
                pltpu.VMEM((total, 2 * depth), jnp.bfloat16),
                pltpu.VMEM((2 * n_rows, 2 * depth), jnp.bfloat16),
            ],
        ),
        out_shape=jax.ShapeDtypeStruct((2, 1, n_rows, total), jnp.float32),
        compiler_params=pltpu.CompilerParams(vmem_limit_bytes=VMEM_VIS),
    )(where, *sources)


def corner_turn(spectrum):
    count, both, span = spectrum.shape
    plane = spectrum.reshape(count // 2, 2, both, span)
    return lax.all_to_all(plane, PLANE, split_axis=0, concat_axis=0, tiled=True)


def along_x(turned):
    x_hi = lax.axis_index("xh")
    mine = lax.dynamic_index_in_dim(turned, x_hi, 1, keepdims=False)
    theirs = lax.dynamic_index_in_dim(turned, 1 - x_hi, 1, keepdims=False)

    def swap(array, far_x, far_t):
        route = [
            (t * 2 + x, (t ^ far_t) * 2 + (x ^ far_x)) for t in range(2) for x in range(2)
        ]
        return lax.ppermute(array, ("ta", "xh"), route)

    both = swap(theirs, 1, 1)
    far = swap(theirs, 1, 0)
    near = swap(mine, 0, 1)
    return [mine, far, near, both]


def local(voltages):
    inputs = voltages.shape[0]
    spectra = voltages.shape[1] // FRAME
    n_time = lax.axis_size("ta")
    n_y, n_z = lax.axis_size("y"), lax.axis_size("z")
    n_chan = n_y * 2 * n_z * 2
    order = np.arange(n_chan).reshape(n_y, 2, n_z, 2).transpose(0, 2, 3, 1).reshape(-1)
    table = jnp.asarray(folded_table(order))
    frames = voltages.reshape(inputs, spectra, FRAME).transpose(1, 0, 2)

    earlier = lax.ppermute(frames[spectra - HALO :], "ta", [(i, i + 1) for i in range(n_time - 1)])
    late = filterbank(frames, 1, frames, BLOCK // HALO - 1, table)
    late, earlier = lax.optimization_barrier((late, earlier))
    turned_late = corner_turn(late)
    early = filterbank(frames, 0, earlier, 0, table)
    sources_late = along_x(turned_late)
    turned_early = corner_turn(early)
    turned_early, *sources_late = lax.optimization_barrier((turned_early, *sources_late))
    sources_early = along_x(turned_early)

    n_rows = inputs * n_chan // n_time
    where = jnp.stack([lax.axis_index("xh"), lax.axis_index("ta") * n_rows]).astype(jnp.int32)
    scale = 1.0 / (16.0 * FRAME * spectra * n_time)
    return visibilities(sources_late + sources_early, where, n_rows, scale)


def solution(mesh):
    fine = Mesh(mesh.devices.reshape(2, 4, 2, 8, 2), ("ta", "y", "xh", "z", "core"))
    gx = ("y", "xh", "z", "core")
    return jax.shard_map(
        local, mesh=fine, in_specs=(P(gx, "ta"),), out_specs=P(None, gx, "ta", None), check_vma=False
    )
```

```python
import functools

import jax
import jax.numpy as jnp
import ml_dtypes
import numpy as np
from jax import lax
from jax.experimental import pallas as pl
from jax.experimental.pallas import tpu as pltpu
from jax.sharding import Mesh
from jax.sharding import PartitionSpec as P

FRAME = 2048
TAPS = 4
UNIT = 64
PIECE = 32
GROUP = 8
HALO = 4
FIRST = 3
DEPTH = 512
N_Y = 4
PLANE = ("y", "z", "core")
COLUMNS = 256
MIB = 1024 * 1024
VMEM_BANK = 56 * MIB
VMEM_VIS = 28 * MIB
F32 = jnp.float32
BF16 = jnp.bfloat16


def pfb_window():
    length = TAPS * FRAME
    points = np.arange(length, dtype=np.float64)
    window = np.sinc((points - length / 2 + 0.5) / FRAME) * (
        0.54 - 0.46 * np.cos(2.0 * np.pi * points / (length - 1))
    )
    return window.reshape(TAPS, FRAME).astype(np.float32)


def dft_table(order):
    phase = (np.arange(FRAME)[:, None] * order[None, :] % FRAME) * (2.0 * np.pi / FRAME)
    return np.concatenate([np.cos(phase), -np.sin(phase)], 1).astype(ml_dtypes.bfloat16)


def filterbank_kernel(first, halo_at, frames, halo, window, table, *refs):
    out, (held, dft, summed, turned, sem) = refs[0], refs[-5:]
    inputs = held.shape[1]
    count = out.shape[0]
    units = out.shape[1] // inputs
    span = PIECE * inputs
    pieces = UNIT // PIECE

    def copy(piece):
        return pltpu.make_async_copy(
            frames.at[pl.ds(first + piece * PIECE, PIECE)],
            held.at[pl.ds(HALO + piece * PIECE, PIECE)],
            sem.at[2 + piece],
        )

    halo_copy = pltpu.make_async_copy(
        halo.at[pl.ds(halo_at, HALO)], held.at[pl.ds(0, HALO)], sem.at[0]
    )
    table_copy = pltpu.make_async_copy(table, dft, sem.at[1])
    halo_copy.start()
    copy(0).start()
    table_copy.start()
    for piece in range(1, units * pieces):
        copy(piece).start()
    halo_copy.wait()

    table_copy.wait()

    def split(piece, lanes):
        high, rest = [], []
        for g in range(PIECE // GROUP):
            at = piece * PIECE + g * GROUP + HALO - TAPS + 1
            some = held[pl.ds(at, GROUP + TAPS - 1), :, lanes].astype(F32)
            total = window[0:1, lanes][None] * some[0:GROUP]
            for k in range(1, TAPS):
                total = total + window[k : k + 1, lanes][None] * some[k : k + GROUP]
            total = total.reshape(GROUP * inputs, DEPTH)
            high.append(total.astype(BF16))
            rest.append((total - high[-1].astype(F32)).astype(BF16))
        return jnp.concatenate(high + rest, 0)

    def body(piece, carry):
        copy(piece).wait()
        product = None
        for n in range(FRAME // DEPTH):
            lanes = slice(n * DEPTH, (n + 1) * DEPTH)
            term = jnp.dot(split(piece, lanes), dft[lanes, :], preferred_element_type=F32)
            product = term if product is None else product + term
        product = product[:span] + product[span:]
        row = pl.multiple_of(lax.rem(piece, pieces) * span, span)
        for part in range(2):
            summed[part, pl.ds(row, span), :] = product[:, part * count : (part + 1) * count]

        @pl.when(lax.rem(piece, pieces) == pieces - 1)
        def _():
            for i in range(inputs):
                both = jnp.concatenate(
                    [summed[part, pl.ds(i, UNIT, stride=inputs), :] for part in range(2)], 0
                )
                row = piece // pieces * inputs + i
                turned[pl.ds(row, count, stride=units * inputs), :] = both.T

        return carry

    lax.fori_loop(0, units * pieces, body, 0)
    out[...] = turned[...].reshape(count, units * inputs, 2 * UNIT).astype(BF16)
    for last in refs[1:-5]:
        last[...] = held[units * UNIT :]


def filterbank(frames, first, spectra, halo, halo_at, window, table, tail):
    _, inputs, _ = frames.shape
    count = table.shape[1] // 2
    units = spectra // UNIT
    there = pl.BlockSpec(memory_space=pl.ANY)
    here = pl.BlockSpec(memory_space=pltpu.VMEM)
    return pl.pallas_call(
        functools.partial(filterbank_kernel, first, halo_at),
        in_specs=[there, there, here, there],
        out_specs=[here] * (1 + tail),
        out_shape=[
            jax.ShapeDtypeStruct((count, units * inputs, 2 * UNIT), BF16),
            jax.ShapeDtypeStruct((HALO, inputs, FRAME), BF16),
        ][: 1 + tail],
        scratch_shapes=[
            pltpu.VMEM((HALO + spectra, inputs, FRAME), BF16),
            pltpu.VMEM(table.shape, BF16),
            pltpu.VMEM((2, UNIT * inputs, count), F32),
            pltpu.VMEM((count * units * inputs, 2 * UNIT), F32),
            pltpu.SemaphoreType.DMA((2 + spectra // PIECE,)),
        ],
        compiler_params=pltpu.CompilerParams(vmem_limit_bytes=VMEM_BANK),
        cost_estimate=pl.CostEstimate(
            flops=4 * spectra * inputs * FRAME * 2 * count,
            bytes_accessed=2 * spectra * inputs * FRAME + MIB,
            transcendentals=0,
        ),
    )(frames, halo, window, table)


def visibility_kernel(inputs, scale, n_sources, where, *refs):
    sources, before = refs[:n_sources], refs[n_sources:-3]
    out, right, left = refs[-3:]
    groups = sources[0].shape[0]
    n_rows = left.shape[0] // 2
    stripe = groups // N_Y * inputs
    units = right.shape[1] // (2 * 2 * UNIT)

    @pl.when(pl.program_id(0) == 0)
    def _():
        for at, source in enumerate(sources):
            per = source.shape[1] // inputs
            wide = source[...].astype(F32).reshape(groups, per, inputs, 2 * UNIT)
            for j in range(per):
                origin, u = (at * per + j) // units, (at * per + j) % units
                x_hi = (where[1] + origin % 2) % 2
                segment = (origin // 2) * units + u
                lanes = slice(segment * 2 * UNIT, (segment + 1) * 2 * UNIT)
                block = wide[:, j].reshape(groups * inputs, 2 * UNIT).astype(BF16)
                for y in range(N_Y):
                    row = pl.multiple_of((2 * y + x_hi) * stripe, stripe)
                    right[pl.ds(row, stripe), lanes] = block[y * stripe : (y + 1) * stripe]
        own = right[pl.ds(pl.multiple_of(where[0], n_rows), n_rows), :]
        left[0:n_rows, :] = own
        lane = lax.broadcasted_iota(jnp.int32, (n_rows, 2 * UNIT), 1)
        for s in range(2 * units):
            lanes = slice(s * 2 * UNIT, (s + 1) * 2 * UNIT)
            swapped = pltpu.roll(own[:, lanes].astype(F32), UNIT, 1)
            left[n_rows:, lanes] = jnp.where(lane < UNIT, swapped, -swapped).astype(BF16)

    at = pl.multiple_of(pl.program_id(0) * COLUMNS, COLUMNS)
    product = lax.dot_general(
        left[...],
        right[pl.ds(at, COLUMNS), :],
        (((1,), (1,)), ((), ())),
        preferred_element_type=F32,
    )
    for part in range(2):
        value = product[part * n_rows : (part + 1) * n_rows]
        if before:
            value = value + before[0][part, 0]
        out[part, 0] = value * scale if scale else value


def visibilities(sources, before, where, inputs, n_rows, scale):
    groups, depth, lanes = sources[0].shape
    total = 2 * groups * inputs
    length = len(sources) * depth // inputs * lanes // 2
    whole = pl.BlockSpec((groups, depth, lanes), lambda r, w: (0, 0, 0))
    block = pl.BlockSpec((2, 1, n_rows, COLUMNS), lambda r, w: (0, 0, 0, r))
    return pl.pallas_call(
        functools.partial(visibility_kernel, inputs, scale, len(sources)),
        grid_spec=pltpu.PrefetchScalarGridSpec(
            num_scalar_prefetch=1,
            grid=(total // COLUMNS,),
            in_specs=[whole] * len(sources) + [block] * len(before),
            out_specs=block,
            scratch_shapes=[
                pltpu.VMEM((total, length), BF16),
                pltpu.VMEM((2 * n_rows, length), BF16),
            ],
        ),
        out_shape=jax.ShapeDtypeStruct((2, 1, n_rows, total), F32),
        compiler_params=pltpu.CompilerParams(vmem_limit_bytes=VMEM_VIS),
        cost_estimate=pl.CostEstimate(
            flops=4 * n_rows * total * length * (1 if scale else 8),
            bytes_accessed=8 * MIB,
            transcendentals=0,
        ),
        input_output_aliases={1 + len(sources): 0} if before else {},
    )(where, *sources, *before)


def swap(array, far_x, far_t):
    route = [(t * 2 + x, (t ^ far_t) * 2 + (x ^ far_x)) for t in range(2) for x in range(2)]
    return lax.ppermute(array, ("ta", "xh"), route)


def along_x(mine, theirs):
    both = swap(theirs, 1, 1)
    far = swap(theirs, 1, 0)
    near = swap(mine, 0, 1)
    return [mine, far, near, both]


def over_plane(array):
    return lax.all_to_all(array, PLANE, split_axis=0, concat_axis=0, tiled=True)


def by_x(array, axis):
    x_hi = lax.axis_index("xh")
    return [lax.dynamic_index_in_dim(array, at, axis, keepdims=False) for at in (x_hi, 1 - x_hi)]


def local(voltages):
    inputs = voltages.shape[0]
    spectra = voltages.shape[1] // FRAME
    n_time = lax.axis_size("ta")
    n_plane = lax.axis_size(PLANE)
    n_chan = 2 * n_plane
    window = jnp.asarray(pfb_window())
    channels = np.arange(n_chan).reshape(N_Y, 2, -1).swapaxes(0, 1)
    x_first = jnp.asarray(dft_table(channels.reshape(-1)))
    x_last = jnp.asarray(dft_table(channels.reshape(2, -1).T.reshape(-1)))
    frames = voltages.reshape(inputs, spectra, FRAME).transpose(1, 0, 2)
    start = spectra // 4 * (4 - FIRST)

    late, last = filterbank(
        frames, start, spectra - start, frames, start - HALO, window, x_last, True
    )
    turned_late = over_plane(late.reshape(n_plane, 2, *late.shape[1:]))
    earlier = lax.ppermute(last, "ta", [(i, i + 1) for i in range(n_time - 1)])
    (early,) = filterbank(frames, 0, start, earlier, 0, window, x_first, False)
    sources_early = along_x(*by_x(early.reshape(2, n_plane, *early.shape[1:]), 0))
    stacked = jnp.concatenate(sources_early, 1)
    turned_late, stacked = lax.optimization_barrier((turned_late, stacked))
    sources_late = along_x(*by_x(turned_late, 1))
    turned_early = over_plane(stacked)

    n_rows = inputs * n_chan // n_time
    where = jnp.stack([lax.axis_index("ta") * n_rows, lax.axis_index("xh")]).astype(jnp.int32)
    scale = 1.0 / (16.0 * FRAME * spectra * n_time)
    so_far = visibilities(sources_late, [], where, inputs, n_rows, None)
    return visibilities([turned_early], [so_far], where, inputs, n_rows, scale)


def solution(mesh):
    fine = Mesh(mesh.devices.reshape(2, 4, 2, 8, 2), ("ta", "y", "xh", "z", "core"))
    gx = ("y", "xh", "z", "core")
    return jax.shard_map(
        local, mesh=fine, in_specs=(P(gx, "ta"),), out_specs=P(None, gx, "ta", None), check_vma=False
    )
```

```python
import functools

import jax
import jax.numpy as jnp
import ml_dtypes
import numpy as np
from jax import lax
from jax.experimental import pallas as pl
from jax.experimental.pallas import tpu as pltpu
from jax.sharding import Mesh
from jax.sharding import PartitionSpec as P

FRAME = 2048
TAPS = 4
UNIT = 64
PIECE = 32
GROUP = 8
HALO = 4
FIRST = 3
DEPTH = 512
N_Y = 4
PLANE = ("y", "z", "core")
BANK_FLOPS = 20 * 1024**3
ROWS_FLOPS = 9 * 1024**3
COLUMNS = 256
MIB = 1024 * 1024
VMEM_BANK = 56 * MIB
VMEM_VIS = 28 * MIB
F32 = jnp.float32
BF16 = jnp.bfloat16


def pfb_window():
    length = TAPS * FRAME
    points = np.arange(length, dtype=np.float64)
    window = np.sinc((points - length / 2 + 0.5) / FRAME) * (
        0.54 - 0.46 * np.cos(2.0 * np.pi * points / (length - 1))
    )
    return window.reshape(TAPS, FRAME).astype(np.float32)


def dft_table(order):
    phase = (np.arange(FRAME)[:, None] * order[None, :] % FRAME) * (2.0 * np.pi / FRAME)
    return np.concatenate([np.cos(phase), -np.sin(phase)], 1).astype(ml_dtypes.bfloat16)


def filterbank_kernel(first, halo_at, frames, halo, window, table, *refs):
    out, (held, dft, summed, turned, sem) = refs[0], refs[-5:]
    inputs = held.shape[1]
    count = out.shape[0]
    units = out.shape[1] // inputs
    span = PIECE * inputs
    pieces = UNIT // PIECE

    def copy(piece):
        return pltpu.make_async_copy(
            frames.at[pl.ds(first + piece * PIECE, PIECE)],
            held.at[pl.ds(HALO + piece * PIECE, PIECE)],
            sem.at[2 + piece],
        )

    halo_copy = pltpu.make_async_copy(
        halo.at[pl.ds(halo_at, HALO)], held.at[pl.ds(0, HALO)], sem.at[0]
    )
    table_copy = pltpu.make_async_copy(table, dft, sem.at[1])
    halo_copy.start()
    copy(0).start()
    table_copy.start()
    for piece in range(1, units * pieces):
        copy(piece).start()
    halo_copy.wait()

    table_copy.wait()

    def split(piece, lanes):
        high, rest = [], []
        for g in range(PIECE // GROUP):
            at = piece * PIECE + g * GROUP + HALO - TAPS + 1
            some = held[pl.ds(at, GROUP + TAPS - 1), :, lanes].astype(F32)
            total = window[0:1, lanes][None] * some[0:GROUP]
            for k in range(1, TAPS):
                total = total + window[k : k + 1, lanes][None] * some[k : k + GROUP]
            total = total.reshape(GROUP * inputs, DEPTH)
            high.append(total.astype(BF16))
            rest.append((total - high[-1].astype(F32)).astype(BF16))
        return jnp.concatenate(high + rest, 0)

    def body(piece, carry):
        copy(piece).wait()
        product = None
        for n in range(FRAME // DEPTH):
            lanes = slice(n * DEPTH, (n + 1) * DEPTH)
            term = jnp.dot(split(piece, lanes), dft[lanes, :], preferred_element_type=F32)
            product = term if product is None else product + term
        product = product[:span] + product[span:]
        row = pl.multiple_of(lax.rem(piece, pieces) * span, span)
        for part in range(2):
            summed[part, pl.ds(row, span), :] = product[:, part * count : (part + 1) * count]

        @pl.when(lax.rem(piece, pieces) == pieces - 1)
        def _():
            for i in range(inputs):
                both = jnp.concatenate(
                    [summed[part, pl.ds(i, UNIT, stride=inputs), :] for part in range(2)], 0
                )
                row = piece // pieces * inputs + i
                turned[pl.ds(row, count, stride=units * inputs), :] = both.T

        return carry

    lax.fori_loop(0, units * pieces, body, 0)
    out[...] = turned[...].reshape(count, units * inputs, 2 * UNIT).astype(BF16)
    for last in refs[1:-5]:
        last[...] = held[units * UNIT :]


def filterbank(frames, first, spectra, halo, halo_at, window, table, tail):
    _, inputs, _ = frames.shape
    count = table.shape[1] // 2
    units = spectra // UNIT
    there = pl.BlockSpec(memory_space=pl.ANY)
    here = pl.BlockSpec(memory_space=pltpu.VMEM)
    return pl.pallas_call(
        functools.partial(filterbank_kernel, first, halo_at),
        in_specs=[there, there, here, there],
        out_specs=[here] * (1 + tail),
        out_shape=[
            jax.ShapeDtypeStruct((count, units * inputs, 2 * UNIT), BF16),
            jax.ShapeDtypeStruct((HALO, inputs, FRAME), BF16),
        ][: 1 + tail],
        scratch_shapes=[
            pltpu.VMEM((HALO + spectra, inputs, FRAME), BF16),
            pltpu.VMEM(table.shape, BF16),
            pltpu.VMEM((2, UNIT * inputs, count), F32),
            pltpu.VMEM((count * units * inputs, 2 * UNIT), F32),
            pltpu.SemaphoreType.DMA((2 + spectra // PIECE,)),
        ],
        compiler_params=pltpu.CompilerParams(vmem_limit_bytes=VMEM_BANK),
        cost_estimate=pl.CostEstimate(
            flops=BANK_FLOPS,
            bytes_accessed=2 * spectra * inputs * FRAME + MIB,
            transcendentals=0,
        ),
    )(frames, halo, window, table)


def rows_kernel(inputs, source, out):
    groups, depth, _ = source.shape
    units = depth // inputs
    wide = source[...].astype(F32).reshape(groups, units, inputs, 2 * UNIT)
    for u in range(units):
        rows = wide[:, u].reshape(groups * inputs, 2 * UNIT).astype(BF16)
        out[u * groups * inputs : (u + 1) * groups * inputs, :] = rows


def as_rows(source, inputs):
    groups, depth, lanes = source.shape
    here = pl.BlockSpec(memory_space=pltpu.VMEM)
    return pl.pallas_call(
        functools.partial(rows_kernel, inputs),
        in_specs=[here],
        out_specs=here,
        out_shape=jax.ShapeDtypeStruct((groups * depth, lanes), BF16),
        compiler_params=pltpu.CompilerParams(vmem_limit_bytes=VMEM_VIS),
        cost_estimate=pl.CostEstimate(flops=ROWS_FLOPS, bytes_accessed=MIB, transcendentals=0),
    )(source)


def visibility_kernel(inputs, scale, where, mine, far, near, both, small, out, right, left):
    groups = mine.shape[0]
    units = mine.shape[1] // inputs
    n_rows = left.shape[0] // 2
    stripe = groups // N_Y * inputs
    n_lanes = 2 * UNIT

    def place(rows, origin, unit):
        x_hi = (where[1] + origin % 2) % 2
        segment = origin // 2 * (units + 1) + unit
        for y in range(N_Y):
            row = pl.multiple_of((2 * y + x_hi) * stripe, stripe)
            right[pl.ds(row, stripe), segment * n_lanes : (segment + 1) * n_lanes] = rows[
                y * stripe : (y + 1) * stripe
            ]

    @pl.when(pl.program_id(0) == 0)
    def _():
        for origin, source in ((0, mine), (2, near), (3, both)):
            wide = source[...].astype(F32).reshape(groups, units, inputs, n_lanes)
            for u in range(units):
                place(wide[:, u].reshape(groups * inputs, n_lanes).astype(BF16), origin, u)
        for u in range(units):
            place(far[u * groups * inputs : (u + 1) * groups * inputs, :], 1, u)
        wide = small[...].astype(F32).reshape(groups, 4, inputs, n_lanes)
        for origin in range(4):
            place(wide[:, origin].reshape(groups * inputs, n_lanes).astype(BF16), origin, units)
        own = right[pl.ds(pl.multiple_of(where[0] * n_rows, n_rows), n_rows), :]
        left[0:n_rows, :] = own
        lane = lax.broadcasted_iota(jnp.int32, (n_rows, n_lanes), 1)
        for s in range(right.shape[1] // n_lanes):
            lanes = slice(s * n_lanes, (s + 1) * n_lanes)
            swapped = pltpu.roll(own[:, lanes].astype(F32), UNIT, 1)
            left[n_rows:, lanes] = jnp.where(lane < UNIT, swapped, -swapped).astype(BF16)

    at = pl.multiple_of(pl.program_id(0) * COLUMNS, COLUMNS)
    product = lax.dot_general(
        left[...],
        right[pl.ds(at, COLUMNS), :],
        (((1,), (1,)), ((), ())),
        preferred_element_type=F32,
    )
    for part in range(2):
        out[part, 0] = product[part * n_rows : (part + 1) * n_rows] * scale


def visibilities(where, sources, inputs, scale):
    groups, depth, lanes = sources[0].shape
    total = 2 * groups * inputs
    length = 2 * (depth // inputs + 1) * lanes
    return pl.pallas_call(
        functools.partial(visibility_kernel, inputs, scale),
        grid_spec=pltpu.PrefetchScalarGridSpec(
            num_scalar_prefetch=1,
            grid=(total // COLUMNS,),
            in_specs=[
                pl.BlockSpec(source.shape, lambda r, w, n=source.ndim: (0,) * n) for source in sources
            ],
            out_specs=pl.BlockSpec((2, 1, total // 2, COLUMNS), lambda r, w: (0, 0, 0, r)),
            scratch_shapes=[pltpu.VMEM((total, length), BF16), pltpu.VMEM((total, length), BF16)],
        ),
        out_shape=jax.ShapeDtypeStruct((2, 1, total // 2, total), F32),
        compiler_params=pltpu.CompilerParams(vmem_limit_bytes=VMEM_VIS),
        cost_estimate=pl.CostEstimate(
            flops=2 * total * total * length, bytes_accessed=7 * MIB, transcendentals=0
        ),
    )(where, *sources)


def swap(array, far_x, far_t):
    route = [(t * 2 + x, (t ^ far_t) * 2 + (x ^ far_x)) for t in range(2) for x in range(2)]
    return lax.ppermute(array, ("ta", "xh"), route)


def along_x(mine, theirs):
    both = swap(theirs, 1, 1)
    far = swap(theirs, 1, 0)
    near = swap(mine, 0, 1)
    return [mine, far, near, both]


def over_plane(array):
    return lax.all_to_all(array, PLANE, split_axis=0, concat_axis=0, tiled=True)


def by_x(array, axis):
    x_hi = lax.axis_index("xh")
    return [lax.dynamic_index_in_dim(array, at, axis, keepdims=False) for at in (x_hi, 1 - x_hi)]


def local(voltages):
    inputs = voltages.shape[0]
    spectra = voltages.shape[1] // FRAME
    n_time = lax.axis_size("ta")
    n_plane = lax.axis_size(PLANE)
    n_chan = 2 * n_plane
    window = jnp.asarray(pfb_window())
    channels = np.arange(n_chan).reshape(N_Y, 2, -1).swapaxes(0, 1)
    x_first = jnp.asarray(dft_table(channels.reshape(-1)))
    x_last = jnp.asarray(dft_table(channels.reshape(2, -1).T.reshape(-1)))
    frames = voltages.reshape(inputs, spectra, FRAME).transpose(1, 0, 2)
    start = spectra // 4 * (4 - FIRST)

    late, last = filterbank(
        frames, start, spectra - start, frames, start - HALO, window, x_last, True
    )
    turned_late = over_plane(late.reshape(n_plane, 2, *late.shape[1:]))
    earlier = lax.ppermute(last, "ta", [(i, i + 1) for i in range(n_time - 1)])
    (early,) = filterbank(frames, 0, start, earlier, 0, window, x_first, False)
    sources_early = along_x(*by_x(early.reshape(2, n_plane, *early.shape[1:]), 0))
    stacked = jnp.concatenate(sources_early, 1)
    turned_late, stacked = lax.optimization_barrier((turned_late, stacked))
    sources_late = along_x(*by_x(turned_late, 1))
    turned_early = over_plane(stacked)

    where = jnp.stack([lax.axis_index("ta"), lax.axis_index("xh")]).astype(jnp.int32)
    scale = 1.0 / (16.0 * FRAME * spectra * n_time)
    mine, far, near, both = sources_late
    far = as_rows(far, inputs)
    return visibilities(where, [mine, far, near, both, turned_early], inputs, scale)


def solution(mesh):
    fine = Mesh(mesh.devices.reshape(2, 4, 2, 8, 2), ("ta", "y", "xh", "z", "core"))
    gx = ("y", "xh", "z", "core")
    return jax.shard_map(
        local, mesh=fine, in_specs=(P(gx, "ta"),), out_specs=P(None, gx, "ta", None), check_vma=False
    )
```

```python
import functools

import jax
import jax.numpy as jnp
import ml_dtypes
import numpy as np
from jax import lax
from jax.experimental import pallas as pl
from jax.experimental.pallas import tpu as pltpu
from jax.sharding import Mesh
from jax.sharding import PartitionSpec as P

FRAME = 2048
TAPS = 4
UNIT = 64
PIECE = 32
GROUP = 8
HALO = 4
FIRST = 3
DEPTH = 512
N_Y = 4
PLANE = ("y", "z", "core")
BANK_FLOPS = 20 * 1024**3
ROWS_FLOPS = 9 * 1024**3
COLUMNS = 512
MIB = 1024 * 1024
VMEM_BANK = 56 * MIB
VMEM_VIS = 28 * MIB
F32 = jnp.float32
BF16 = jnp.bfloat16


def pfb_window():
    length = TAPS * FRAME
    points = np.arange(length, dtype=np.float64)
    window = np.sinc((points - length / 2 + 0.5) / FRAME) * (
        0.54 - 0.46 * np.cos(2.0 * np.pi * points / (length - 1))
    )
    return window.reshape(TAPS, FRAME).astype(np.float32)


def dft_table(order):
    phase = (np.arange(FRAME)[:, None] * order[None, :] % FRAME) * (2.0 * np.pi / FRAME)
    return np.concatenate([np.cos(phase), -np.sin(phase)], 1).astype(ml_dtypes.bfloat16)


def filterbank_kernel(first, halo_at, frames, halo, window, table, *refs):
    out, (held, weight, dft, summed, turned, sem) = refs[0], refs[-6:]
    inputs = held.shape[1]
    count = out.shape[0]
    units = out.shape[1] // inputs
    span = PIECE * inputs
    pieces = UNIT // PIECE

    def copy(piece):
        return pltpu.make_async_copy(
            frames.at[pl.ds(first + piece * PIECE, PIECE)],
            held.at[pl.ds(HALO + piece * PIECE, PIECE)],
            sem.at[3 + piece],
        )

    halo_copy = pltpu.make_async_copy(
        halo.at[pl.ds(halo_at, HALO)], held.at[pl.ds(0, HALO)], sem.at[0]
    )
    table_copy = pltpu.make_async_copy(table, dft, sem.at[1])
    window_copy = pltpu.make_async_copy(window, weight, sem.at[2])
    window_copy.start()
    halo_copy.start()
    copy(0).start()
    table_copy.start()
    for piece in range(1, units * pieces):
        copy(piece).start()
    window_copy.wait()
    halo_copy.wait()

    table_copy.wait()

    def split(piece, lanes):
        high, rest = [], []
        for g in range(PIECE // GROUP):
            at = piece * PIECE + g * GROUP + HALO - TAPS + 1
            some = held[pl.ds(at, GROUP + TAPS - 1), :, lanes].astype(F32)
            total = weight[0:1, lanes][None] * some[0:GROUP]
            for k in range(1, TAPS):
                total = total + weight[k : k + 1, lanes][None] * some[k : k + GROUP]
            total = total.reshape(GROUP * inputs, DEPTH)
            high.append(total.astype(BF16))
            rest.append((total - high[-1].astype(F32)).astype(BF16))
        return jnp.concatenate(high + rest, 0)

    def turn(u, i):
        both = jnp.concatenate(
            [summed[lax.rem(u, 2), part, pl.ds(i, UNIT, stride=inputs), :] for part in range(2)], 0
        )
        turned[pl.ds(u * inputs + i, count, stride=units * inputs), :] = both.T

    def body(piece, carry):
        copy(piece).wait()
        u, step = piece // pieces, lax.rem(piece, pieces)
        for i in range(inputs // pieces):
            turn(jnp.maximum(u - 1, 0), step * (inputs // pieces) + i)
        product = None
        for n in range(FRAME // DEPTH):
            lanes = slice(n * DEPTH, (n + 1) * DEPTH)
            term = jnp.dot(split(piece, lanes), dft[lanes, :], preferred_element_type=F32)
            product = term if product is None else product + term
        product = product[:span] + product[span:]
        row = pl.multiple_of(step * span, span)
        for part in range(2):
            summed[lax.rem(u, 2), part, pl.ds(row, span), :] = product[
                :, part * count : (part + 1) * count
            ]
        return carry

    lax.fori_loop(0, units * pieces, body, 0)
    for i in range(inputs):
        turn(units - 1, i)
    out[...] = turned[...].reshape(count, units * inputs, 2 * UNIT).astype(BF16)
    for last in refs[1:-6]:
        last[...] = held[units * UNIT :]


def filterbank(frames, first, spectra, halo, halo_at, window, table, tail):
    _, inputs, _ = frames.shape
    count = table.shape[1] // 2
    units = spectra // UNIT
    there = pl.BlockSpec(memory_space=pl.ANY)
    here = pl.BlockSpec(memory_space=pltpu.VMEM)
    return pl.pallas_call(
        functools.partial(filterbank_kernel, first, halo_at),
        in_specs=[there] * 4,
        out_specs=[here] * (1 + tail),
        out_shape=[
            jax.ShapeDtypeStruct((count, units * inputs, 2 * UNIT), BF16),
            jax.ShapeDtypeStruct((HALO, inputs, FRAME), BF16),
        ][: 1 + tail],
        scratch_shapes=[
            pltpu.VMEM((HALO + spectra, inputs, FRAME), BF16),
            pltpu.VMEM(window.shape, F32),
            pltpu.VMEM(table.shape, BF16),
            pltpu.VMEM((2, 2, UNIT * inputs, count), F32),
            pltpu.VMEM((count * units * inputs, 2 * UNIT), F32),
            pltpu.SemaphoreType.DMA((3 + spectra // PIECE,)),
        ],
        compiler_params=pltpu.CompilerParams(vmem_limit_bytes=VMEM_BANK),
        cost_estimate=pl.CostEstimate(
            flops=BANK_FLOPS,
            bytes_accessed=2 * spectra * inputs * FRAME + MIB,
            transcendentals=0,
        ),
    )(frames, halo, window, table)


def rows_kernel(inputs, source, out):
    groups, depth, _ = source.shape
    units = depth // inputs
    wide = source[...].astype(F32).reshape(groups, units, inputs, 2 * UNIT)
    for u in range(units):
        rows = wide[:, u].reshape(groups * inputs, 2 * UNIT).astype(BF16)
        out[u * groups * inputs : (u + 1) * groups * inputs, :] = rows


def as_rows(source, inputs):
    groups, depth, lanes = source.shape
    here = pl.BlockSpec(memory_space=pltpu.VMEM)
    return pl.pallas_call(
        functools.partial(rows_kernel, inputs),
        in_specs=[here],
        out_specs=here,
        out_shape=jax.ShapeDtypeStruct((groups * depth, lanes), BF16),
        compiler_params=pltpu.CompilerParams(vmem_limit_bytes=VMEM_VIS),
        cost_estimate=pl.CostEstimate(flops=ROWS_FLOPS, bytes_accessed=MIB, transcendentals=0),
    )(source)


def visibility_kernel(inputs, scale, where, mine, far, near, both, small, out, right, left):
    groups = mine.shape[0]
    units = mine.shape[1] // inputs
    n_rows = left.shape[0] // 2
    stripe = groups // N_Y * inputs
    n_lanes = 2 * UNIT

    def place(rows, origin, unit):
        x_hi = (where[1] + origin % 2) % 2
        segment = origin // 2 * (units + 1) + unit
        for y in range(N_Y):
            row = pl.multiple_of((2 * y + x_hi) * stripe, stripe)
            right[pl.ds(row, stripe), segment * n_lanes : (segment + 1) * n_lanes] = rows[
                y * stripe : (y + 1) * stripe
            ]

    @pl.when(pl.program_id(0) == 0)
    def _():
        for origin, source in ((0, mine), (2, near), (3, both)):
            wide = source[...].astype(F32).reshape(groups, units, inputs, n_lanes)
            for u in range(units):
                place(wide[:, u].reshape(groups * inputs, n_lanes).astype(BF16), origin, u)
        for u in range(units):
            place(far[u * groups * inputs : (u + 1) * groups * inputs, :], 1, u)
        wide = small[...].astype(F32).reshape(groups, 4, inputs, n_lanes)
        for origin in range(4):
            place(wide[:, origin].reshape(groups * inputs, n_lanes).astype(BF16), origin, units)
        own = right[pl.ds(pl.multiple_of(where[0] * n_rows, n_rows), n_rows), :]
        left[0:n_rows, :] = own
        lane = lax.broadcasted_iota(jnp.int32, (n_rows, n_lanes), 1)
        for s in range(right.shape[1] // n_lanes):
            lanes = slice(s * n_lanes, (s + 1) * n_lanes)
            swapped = pltpu.roll(own[:, lanes].astype(F32), UNIT, 1)
            left[n_rows:, lanes] = jnp.where(lane < UNIT, swapped, -swapped).astype(BF16)

    at = pl.multiple_of(pl.program_id(0) * COLUMNS, COLUMNS)
    product = lax.dot_general(
        left[...],
        right[pl.ds(at, COLUMNS), :],
        (((1,), (1,)), ((), ())),
        preferred_element_type=F32,
    )
    for part in range(2):
        out[part, 0] = product[part * n_rows : (part + 1) * n_rows] * scale


def visibilities(where, sources, inputs, scale):
    groups, depth, lanes = sources[0].shape
    total = 2 * groups * inputs
    length = 2 * (depth // inputs + 1) * lanes
    return pl.pallas_call(
        functools.partial(visibility_kernel, inputs, scale),
        grid_spec=pltpu.PrefetchScalarGridSpec(
            num_scalar_prefetch=1,
            grid=(total // COLUMNS,),
            in_specs=[
                pl.BlockSpec(source.shape, lambda r, w, n=source.ndim: (0,) * n) for source in sources
            ],
            out_specs=pl.BlockSpec((2, 1, total // 2, COLUMNS), lambda r, w: (0, 0, 0, r)),
            scratch_shapes=[pltpu.VMEM((total, length), BF16), pltpu.VMEM((total, length), BF16)],
        ),
        out_shape=jax.ShapeDtypeStruct((2, 1, total // 2, total), F32),
        compiler_params=pltpu.CompilerParams(vmem_limit_bytes=VMEM_VIS),
        cost_estimate=pl.CostEstimate(
            flops=2 * total * total * length, bytes_accessed=7 * MIB, transcendentals=0
        ),
    )(where, *sources)


def swap(array, far_x, far_t):
    route = [(t * 2 + x, (t ^ far_t) * 2 + (x ^ far_x)) for t in range(2) for x in range(2)]
    return lax.ppermute(array, ("ta", "xh"), route)


def along_x(mine, theirs):
    both = swap(theirs, 1, 1)
    far = swap(theirs, 1, 0)
    near = swap(mine, 0, 1)
    return [mine, far, near, both]


def over_plane(array):
    return lax.all_to_all(array, PLANE, split_axis=0, concat_axis=0, tiled=True)


def by_x(array, axis):
    x_hi = lax.axis_index("xh")
    return [lax.dynamic_index_in_dim(array, at, axis, keepdims=False) for at in (x_hi, 1 - x_hi)]


def local(voltages):
    inputs = voltages.shape[0]
    spectra = voltages.shape[1] // FRAME
    n_time = lax.axis_size("ta")
    n_plane = lax.axis_size(PLANE)
    n_chan = 2 * n_plane
    window = jnp.asarray(pfb_window())
    channels = np.arange(n_chan).reshape(N_Y, 2, -1).swapaxes(0, 1)
    x_first = jnp.asarray(dft_table(channels.reshape(-1)))
    x_last = jnp.asarray(dft_table(channels.reshape(2, -1).T.reshape(-1)))
    frames = voltages.reshape(inputs, spectra, FRAME).transpose(1, 0, 2)
    start = spectra // 4 * (4 - FIRST)

    late, last = filterbank(
        frames, start, spectra - start, frames, start - HALO, window, x_last, True
    )
    turned_late = over_plane(late.reshape(n_plane, 2, *late.shape[1:]))
    earlier = lax.ppermute(last, "ta", [(i, i + 1) for i in range(n_time - 1)])
    (early,) = filterbank(frames, 0, start, earlier, 0, window, x_first, False)
    sources_early = along_x(*by_x(early.reshape(2, n_plane, *early.shape[1:]), 0))
    stacked = jnp.concatenate(sources_early, 1)
    turned_late, stacked = lax.optimization_barrier((turned_late, stacked))
    sources_late = along_x(*by_x(turned_late, 1))
    turned_early = over_plane(stacked)

    where = jnp.stack([lax.axis_index("ta"), lax.axis_index("xh")]).astype(jnp.int32)
    scale = 1.0 / (16.0 * FRAME * spectra * n_time)
    mine, far, near, both = sources_late
    far = as_rows(far, inputs)
    return visibilities(where, [mine, far, near, both, turned_early], inputs, scale)


def solution(mesh):
    fine = Mesh(mesh.devices.reshape(2, 4, 2, 8, 2), ("ta", "y", "xh", "z", "core"))
    gx = ("y", "xh", "z", "core")
    return jax.shard_map(
        local, mesh=fine, in_specs=(P(gx, "ta"),), out_specs=P(None, gx, "ta", None), check_vma=False
    )
```

```python
import functools

import jax
import jax.numpy as jnp
import ml_dtypes
import numpy as np
from jax import lax
from jax.experimental import pallas as pl
from jax.experimental.pallas import tpu as pltpu
from jax.sharding import Mesh
from jax.sharding import PartitionSpec as P

FRAME = 2048
TAPS = 4
UNIT = 64
PIECE = 32
GROUP = 8
HALO = 4
FIRST = 3
DEPTH = 512
N_Y = 4
PLANE = ("y", "z", "core")
BANK_FLOPS = 20 * 1024**3
ROWS_FLOPS = 9 * 1024**3
COLUMNS = 512
MIB = 1024 * 1024
VMEM_BANK = 56 * MIB
VMEM_VIS = 28 * MIB
F32 = jnp.float32
BF16 = jnp.bfloat16


def pfb_window():
    length = TAPS * FRAME
    points = np.arange(length, dtype=np.float64)
    window = np.sinc((points - length / 2 + 0.5) / FRAME) * (
        0.54 - 0.46 * np.cos(2.0 * np.pi * points / (length - 1))
    )
    return window.reshape(TAPS, FRAME).astype(np.float32)


def dft_table(order):
    phase = (np.arange(FRAME)[:, None] * order[None, :] % FRAME) * (2.0 * np.pi / FRAME)
    return np.concatenate([np.cos(phase), -np.sin(phase)], 1).astype(ml_dtypes.bfloat16)


def filterbank_kernel(first, halo_at, frames, halo, window, table, *refs):
    out, (held, weight, dft, summed, turned, sem) = refs[0], refs[-6:]
    inputs = held.shape[1]
    count = out.shape[0]
    units = out.shape[1] // inputs
    span = PIECE * inputs
    pieces = UNIT // PIECE

    def copy(piece):
        return pltpu.make_async_copy(
            frames.at[pl.ds(first + piece * PIECE, PIECE)],
            held.at[pl.ds(HALO + piece * PIECE, PIECE)],
            sem.at[3 + piece],
        )

    halo_copy = pltpu.make_async_copy(
        halo.at[pl.ds(halo_at, HALO)], held.at[pl.ds(0, HALO)], sem.at[0]
    )
    table_copy = pltpu.make_async_copy(table, dft, sem.at[1])
    window_copy = pltpu.make_async_copy(window, weight, sem.at[2])
    window_copy.start()
    halo_copy.start()
    copy(0).start()
    table_copy.start()
    for piece in range(1, units * pieces):
        copy(piece).start()
    window_copy.wait()
    halo_copy.wait()

    table_copy.wait()

    def split(piece, lanes):
        high, rest = [], []
        for g in range(PIECE // GROUP):
            at = piece * PIECE + g * GROUP + HALO - TAPS + 1
            some = held[pl.ds(at, GROUP + TAPS - 1), :, lanes].astype(F32)
            total = weight[0:1, lanes][None] * some[0:GROUP]
            for k in range(1, TAPS):
                total = total + weight[k : k + 1, lanes][None] * some[k : k + GROUP]
            total = total.reshape(GROUP * inputs, DEPTH)
            high.append(total.astype(BF16))
            rest.append((total - high[-1].astype(F32)).astype(BF16))
        return jnp.concatenate(high + rest, 0)

    def turn(u, i):
        both = jnp.concatenate(
            [summed[lax.rem(u, 2), part, pl.ds(i, UNIT, stride=inputs), :] for part in range(2)], 0
        )
        turned[pl.ds(u * inputs + i, count, stride=units * inputs), :] = both.T

    def body(piece, carry):
        copy(piece).wait()
        u, step = piece // pieces, lax.rem(piece, pieces)
        for i in range(inputs // pieces):
            turn(jnp.maximum(u - 1, 0), step * (inputs // pieces) + i)
        product = None
        for n in range(FRAME // DEPTH):
            lanes = slice(n * DEPTH, (n + 1) * DEPTH)
            term = jnp.dot(split(piece, lanes), dft[lanes, :], preferred_element_type=F32)
            product = term if product is None else product + term
        product = product[:span] + product[span:]
        row = pl.multiple_of(step * span, span)
        for part in range(2):
            summed[lax.rem(u, 2), part, pl.ds(row, span), :] = product[
                :, part * count : (part + 1) * count
            ]
        return carry

    lax.fori_loop(0, units * pieces, body, 0)
    for i in range(inputs):
        turn(units - 1, i)
    out[...] = turned[...].reshape(count, units * inputs, 2 * UNIT).astype(BF16)
    for last in refs[1:-6]:
        last[...] = held[units * UNIT :]


def filterbank(frames, first, spectra, halo, halo_at, window, table, tail):
    _, inputs, _ = frames.shape
    count = table.shape[1] // 2
    units = spectra // UNIT
    there = pl.BlockSpec(memory_space=pl.ANY)
    here = pl.BlockSpec(memory_space=pltpu.VMEM)
    return pl.pallas_call(
        functools.partial(filterbank_kernel, first, halo_at),
        in_specs=[there] * 4,
        out_specs=[here] * (1 + tail),
        out_shape=[
            jax.ShapeDtypeStruct((count, units * inputs, 2 * UNIT), BF16),
            jax.ShapeDtypeStruct((HALO, inputs, FRAME), BF16),
        ][: 1 + tail],
        scratch_shapes=[
            pltpu.VMEM((HALO + spectra, inputs, FRAME), BF16),
            pltpu.VMEM(window.shape, F32),
            pltpu.VMEM(table.shape, BF16),
            pltpu.VMEM((2, 2, UNIT * inputs, count), F32),
            pltpu.VMEM((count * units * inputs, 2 * UNIT), F32),
            pltpu.SemaphoreType.DMA((3 + spectra // PIECE,)),
        ],
        compiler_params=pltpu.CompilerParams(vmem_limit_bytes=VMEM_BANK),
        cost_estimate=pl.CostEstimate(
            flops=BANK_FLOPS,
            bytes_accessed=2 * spectra * inputs * FRAME + MIB,
            transcendentals=0,
        ),
    )(frames, halo, window, table)


def rows_kernel(inputs, source, out):
    groups, depth, _ = source.shape
    units = depth // inputs
    wide = source[...].astype(F32).reshape(groups, units, inputs, 2 * UNIT)
    for u in range(units):
        rows = wide[:, u].reshape(groups * inputs, 2 * UNIT).astype(BF16)
        out[u * groups * inputs : (u + 1) * groups * inputs, :] = rows


def as_rows(source, inputs):
    groups, depth, lanes = source.shape
    here = pl.BlockSpec(memory_space=pltpu.VMEM)
    return pl.pallas_call(
        functools.partial(rows_kernel, inputs),
        in_specs=[here],
        out_specs=here,
        out_shape=jax.ShapeDtypeStruct((groups * depth, lanes), BF16),
        compiler_params=pltpu.CompilerParams(vmem_limit_bytes=VMEM_VIS),
        cost_estimate=pl.CostEstimate(flops=ROWS_FLOPS, bytes_accessed=MIB, transcendentals=0),
    )(source)


def visibility_kernel(inputs, scale, where, mine, far, near, both, small, out, right, left):
    groups = mine.shape[0]
    units = mine.shape[1] // inputs
    n_rows = left.shape[0] // 2
    stripe = groups // N_Y * inputs
    n_lanes = 2 * UNIT

    def place(rows, origin, unit):
        x_hi = (where[1] + origin % 2) % 2
        segment = origin // 2 * (units + 1) + unit
        for y in range(N_Y):
            row = pl.multiple_of((2 * y + x_hi) * stripe, stripe)
            right[pl.ds(row, stripe), segment * n_lanes : (segment + 1) * n_lanes] = rows[
                y * stripe : (y + 1) * stripe
            ]

    @pl.when(pl.program_id(0) == 0)
    def _():
        for origin, source in ((0, mine), (2, near), (3, both)):
            wide = source[...].astype(F32).reshape(groups, units, inputs, n_lanes)
            for u in range(units):
                place(wide[:, u].reshape(groups * inputs, n_lanes).astype(BF16), origin, u)
        for u in range(units):
            place(far[u * groups * inputs : (u + 1) * groups * inputs, :], 1, u)
        wide = small[...].astype(F32).reshape(groups, 4, inputs, n_lanes)
        for origin in range(4):
            place(wide[:, origin].reshape(groups * inputs, n_lanes).astype(BF16), origin, units)
        own = right[pl.ds(pl.multiple_of(where[0] * n_rows, n_rows), n_rows), :]
        left[0:n_rows, :] = own
        lane = lax.broadcasted_iota(jnp.int32, (n_rows, n_lanes), 1)
        for s in range(right.shape[1] // n_lanes):
            lanes = slice(s * n_lanes, (s + 1) * n_lanes)
            swapped = pltpu.roll(own[:, lanes].astype(F32), UNIT, 1)
            left[n_rows:, lanes] = jnp.where(lane < UNIT, swapped, -swapped).astype(BF16)

    at = pl.multiple_of(pl.program_id(0) * COLUMNS, COLUMNS)
    product = lax.dot_general(
        left[...],
        right[pl.ds(at, COLUMNS), :],
        (((1,), (1,)), ((), ())),
        preferred_element_type=F32,
    )
    for part in range(2):
        out[part, 0] = product[part * n_rows : (part + 1) * n_rows] * scale


def visibilities(where, sources, inputs, scale):
    groups, depth, lanes = sources[0].shape
    total = 2 * groups * inputs
    length = 2 * (depth // inputs + 1) * lanes
    return pl.pallas_call(
        functools.partial(visibility_kernel, inputs, scale),
        grid_spec=pltpu.PrefetchScalarGridSpec(
            num_scalar_prefetch=1,
            grid=(total // COLUMNS,),
            in_specs=[
                pl.BlockSpec(source.shape, lambda r, w, n=source.ndim: (0,) * n) for source in sources
            ],
            out_specs=pl.BlockSpec((2, 1, total // 2, COLUMNS), lambda r, w: (0, 0, 0, r)),
            scratch_shapes=[pltpu.VMEM((total, length), BF16), pltpu.VMEM((total, length), BF16)],
        ),
        out_shape=jax.ShapeDtypeStruct((2, 1, total // 2, total), F32),
        compiler_params=pltpu.CompilerParams(vmem_limit_bytes=VMEM_VIS),
        cost_estimate=pl.CostEstimate(
            flops=2 * total * total * length, bytes_accessed=7 * MIB, transcendentals=0
        ),
    )(where, *sources)


def swap(array, far_x, far_t):
    route = [(t * 2 + x, (t ^ far_t) * 2 + (x ^ far_x)) for t in range(2) for x in range(2)]
    return lax.ppermute(array, ("ta", "xh"), route)


def along_x(mine, theirs):
    both = swap(theirs, 1, 1)
    far = swap(theirs, 1, 0)
    near = swap(mine, 0, 1)
    return [mine, far, near, both]


def over_plane(array):
    return lax.all_to_all(array, PLANE, split_axis=0, concat_axis=0, tiled=True)


def by_x(array, axis):
    x_hi = lax.axis_index("xh")
    return [lax.dynamic_index_in_dim(array, at, axis, keepdims=False) for at in (x_hi, 1 - x_hi)]


def local(voltages):
    inputs = voltages.shape[0]
    spectra = voltages.shape[1] // FRAME
    n_time = lax.axis_size("ta")
    n_plane = lax.axis_size(PLANE)
    n_chan = 2 * n_plane
    window = jnp.asarray(pfb_window())
    channels = np.arange(n_chan).reshape(N_Y, 2, -1).swapaxes(0, 1)
    x_first = jnp.asarray(dft_table(channels.reshape(-1)))
    x_last = jnp.asarray(dft_table(channels.reshape(2, -1).T.reshape(-1)))
    frames = voltages.reshape(inputs, spectra, FRAME).transpose(1, 0, 2)
    start = spectra // 4 * (4 - FIRST)

    late, last = filterbank(
        frames, start, spectra - start, frames, start - HALO, window, x_last, True
    )
    turned_late = over_plane(late.reshape(n_plane, 2, *late.shape[1:]))
    earlier = lax.ppermute(last, "ta", [(i, (i + 1) % n_time) for i in range(n_time)])
    earlier = jnp.where(lax.axis_index("ta") == 0, jnp.zeros_like(earlier), earlier)
    (early,) = filterbank(frames, 0, start, earlier, 0, window, x_first, False)
    sources_early = along_x(*by_x(early.reshape(2, n_plane, *early.shape[1:]), 0))
    stacked = jnp.concatenate(sources_early, 1)
    turned_late, stacked = lax.optimization_barrier((turned_late, stacked))
    sources_late = along_x(*by_x(turned_late, 1))
    turned_early = over_plane(stacked)

    where = jnp.stack([lax.axis_index("ta"), lax.axis_index("xh")]).astype(jnp.int32)
    scale = 1.0 / (16.0 * FRAME * spectra * n_time)
    mine, far, near, both = sources_late
    far = as_rows(far, inputs)
    return visibilities(where, [mine, far, near, both, turned_early], inputs, scale)


def solution(mesh):
    fine = Mesh(mesh.devices.reshape(2, 4, 2, 8, 2), ("ta", "y", "xh", "z", "core"))
    gx = ("y", "xh", "z", "core")
    return jax.shard_map(
        local, mesh=fine, in_specs=(P(gx, "ta"),), out_specs=P(None, gx, "ta", None), check_vma=False
    )
```

```python
import functools

import jax
import jax.numpy as jnp
import ml_dtypes
import numpy as np
from jax import lax
from jax.experimental import pallas as pl
from jax.experimental.pallas import tpu as pltpu
from jax.sharding import Mesh
from jax.sharding import PartitionSpec as P

FRAME = 2048
TAPS = 4
UNIT = 64
PIECE = 32
GROUP = 8
HALO = 4
FIRST = 3
DEPTH = 512
N_Y = 4
PLANE = ("y", "z", "core")
BANK_FLOPS = 20 * 1024**3
ROWS_FLOPS = 9 * 1024**3
COLUMNS = 512
MIB = 1024 * 1024
VMEM_BANK = 56 * MIB
VMEM_VIS = 28 * MIB
F32 = jnp.float32
BF16 = jnp.bfloat16


def pfb_window():
    length = TAPS * FRAME
    points = np.arange(length, dtype=np.float64)
    window = np.sinc((points - length / 2 + 0.5) / FRAME) * (
        0.54 - 0.46 * np.cos(2.0 * np.pi * points / (length - 1))
    )
    return window.reshape(TAPS, FRAME).astype(np.float32)


def dft_table(order):
    phase = (np.arange(FRAME)[:, None] * order[None, :] % FRAME) * (2.0 * np.pi / FRAME)
    return np.concatenate([np.cos(phase), -np.sin(phase)], 1).astype(ml_dtypes.bfloat16)


def filterbank_kernel(first, halo_at, frames, halo, window, table, *refs):
    out, (held, weight, dft, summed, turned, sem) = refs[0], refs[-6:]
    inputs = held.shape[1]
    count = out.shape[0]
    units = out.shape[1] // inputs
    span = PIECE * inputs
    pieces = UNIT // PIECE

    def copy(piece):
        return pltpu.make_async_copy(
            frames.at[pl.ds(first + piece * PIECE, PIECE)],
            held.at[pl.ds(HALO + piece * PIECE, PIECE)],
            sem.at[3 + piece],
        )

    halo_copy = pltpu.make_async_copy(
        halo.at[pl.ds(halo_at, HALO)], held.at[pl.ds(0, HALO)], sem.at[0]
    )
    table_copy = pltpu.make_async_copy(table, dft, sem.at[1])
    window_copy = pltpu.make_async_copy(window, weight, sem.at[2])
    window_copy.start()
    halo_copy.start()
    copy(0).start()
    table_copy.start()
    for piece in range(1, units * pieces):
        copy(piece).start()
    window_copy.wait()
    halo_copy.wait()

    table_copy.wait()

    def split(piece, lanes):
        high, rest = [], []
        for g in range(PIECE // GROUP):
            at = piece * PIECE + g * GROUP + HALO - TAPS + 1
            some = held[pl.ds(at, GROUP + TAPS - 1), :, lanes].astype(F32)
            total = weight[0:1, lanes][None] * some[0:GROUP]
            for k in range(1, TAPS):
                total = total + weight[k : k + 1, lanes][None] * some[k : k + GROUP]
            total = total.reshape(GROUP * inputs, DEPTH)
            high.append(total.astype(BF16))
            rest.append((total - high[-1].astype(F32)).astype(BF16))
        return jnp.concatenate(high + rest, 0)

    def turn(u, i):
        both = jnp.concatenate(
            [summed[lax.rem(u, 2), part, pl.ds(i, UNIT, stride=inputs), :] for part in range(2)], 0
        )
        turned[pl.ds(u * inputs + i, count, stride=units * inputs), :] = both.T

    def body(piece, carry):
        copy(piece).wait()
        u, step = piece // pieces, lax.rem(piece, pieces)
        for i in range(inputs // pieces):
            turn(jnp.maximum(u - 1, 0), step * (inputs // pieces) + i)
        product = None
        for n in range(FRAME // DEPTH):
            lanes = slice(n * DEPTH, (n + 1) * DEPTH)
            term = jnp.dot(split(piece, lanes), dft[lanes, :], preferred_element_type=F32)
            product = term if product is None else product + term
        product = product[:span] + product[span:]
        row = pl.multiple_of(step * span, span)
        for part in range(2):
            summed[lax.rem(u, 2), part, pl.ds(row, span), :] = product[
                :, part * count : (part + 1) * count
            ]
        return carry

    lax.fori_loop(0, units * pieces, body, 0)
    for i in range(inputs):
        turn(units - 1, i)
    out[...] = turned[...].reshape(count, units * inputs, 2 * UNIT).astype(BF16)
    for last in refs[1:-6]:
        last[...] = held[units * UNIT :]


def filterbank(frames, first, spectra, halo, halo_at, window, table, tail):
    _, inputs, _ = frames.shape
    count = table.shape[1] // 2
    units = spectra // UNIT
    there = pl.BlockSpec(memory_space=pl.ANY)
    here = pl.BlockSpec(memory_space=pltpu.VMEM)
    return pl.pallas_call(
        functools.partial(filterbank_kernel, first, halo_at),
        in_specs=[there] * 4,
        out_specs=[here] * (1 + tail),
        out_shape=[
            jax.ShapeDtypeStruct((count, units * inputs, 2 * UNIT), BF16),
            jax.ShapeDtypeStruct((HALO, inputs, FRAME), BF16),
        ][: 1 + tail],
        scratch_shapes=[
            pltpu.VMEM((HALO + spectra, inputs, FRAME), BF16),
            pltpu.VMEM(window.shape, F32),
            pltpu.VMEM(table.shape, BF16),
            pltpu.VMEM((2, 2, UNIT * inputs, count), F32),
            pltpu.VMEM((count * units * inputs, 2 * UNIT), F32),
            pltpu.SemaphoreType.DMA((3 + spectra // PIECE,)),
        ],
        compiler_params=pltpu.CompilerParams(vmem_limit_bytes=VMEM_BANK),
        cost_estimate=pl.CostEstimate(
            flops=BANK_FLOPS,
            bytes_accessed=2 * spectra * inputs * FRAME + MIB,
            transcendentals=0,
        ),
    )(frames, halo, window, table)


def rows_kernel(inputs, source, out):
    groups, depth, _ = source.shape
    units = depth // inputs
    wide = source[...].astype(F32).reshape(groups, units, inputs, 2 * UNIT)
    for u in range(units):
        rows = wide[:, u].reshape(groups * inputs, 2 * UNIT).astype(BF16)
        out[u * groups * inputs : (u + 1) * groups * inputs, :] = rows


def as_rows(source, inputs):
    groups, depth, lanes = source.shape
    here = pl.BlockSpec(memory_space=pltpu.VMEM)
    return pl.pallas_call(
        functools.partial(rows_kernel, inputs),
        in_specs=[here],
        out_specs=here,
        out_shape=jax.ShapeDtypeStruct((groups * depth, lanes), BF16),
        compiler_params=pltpu.CompilerParams(vmem_limit_bytes=VMEM_VIS),
        cost_estimate=pl.CostEstimate(flops=ROWS_FLOPS, bytes_accessed=MIB, transcendentals=0),
    )(source)


def visibility_kernel(inputs, scale, where, mine, far, near, both, small, out, right, left, ready, sem):
    groups = mine.shape[0]
    units = mine.shape[1] // inputs
    n_rows = left.shape[0]
    stripe = groups // N_Y * inputs
    n_lanes = 2 * UNIT

    def place(rows, origin, unit):
        x_hi = (where[1] + origin % 2) % 2
        segment = origin // 2 * (units + 1) + unit
        for y in range(N_Y):
            row = pl.multiple_of((2 * y + x_hi) * stripe, stripe)
            right[pl.ds(row, stripe), segment * n_lanes : (segment + 1) * n_lanes] = rows[
                y * stripe : (y + 1) * stripe
            ]

    for origin, source in ((0, mine), (2, near), (3, both)):
        wide = source[...].astype(F32).reshape(groups, units, inputs, n_lanes)
        for u in range(units):
            place(wide[:, u].reshape(groups * inputs, n_lanes).astype(BF16), origin, u)
    for u in range(units):
        place(far[u * groups * inputs : (u + 1) * groups * inputs, :], 1, u)
    wide = small[...].astype(F32).reshape(groups, 4, inputs, n_lanes)
    for origin in range(4):
        place(wide[:, origin].reshape(groups * inputs, n_lanes).astype(BF16), origin, units)
    own = pl.ds(pl.multiple_of(where[0] * n_rows, n_rows), n_rows)
    lane = lax.broadcasted_iota(jnp.int32, (n_rows, n_lanes), 1)
    copies = []
    for part in range(2):
        if part == 1:
            for s in range(right.shape[1] // n_lanes):
                lanes = slice(s * n_lanes, (s + 1) * n_lanes)
                swapped = pltpu.roll(right[own, lanes].astype(F32), UNIT, 1)
                left[:, lanes] = jnp.where(lane < UNIT, swapped, -swapped).astype(BF16)
        for block in range(right.shape[0] // COLUMNS):
            columns = slice(block * COLUMNS, (block + 1) * COLUMNS)
            product = lax.dot_general(
                left[...] if part else right[own, :],
                right[columns, :],
                (((1,), (1,)), ((), ())),
                preferred_element_type=F32,
            )
            ready[block, part] = product * scale
            copies.append(
                pltpu.make_async_copy(
                    ready.at[block, part], out.at[part, 0, :, columns], sem.at[block, part]
                )
            )
            copies[-1].start()
    for copy in copies:
        copy.wait()


def visibilities(where, sources, inputs, scale):
    groups, depth, lanes = sources[0].shape
    total = 2 * groups * inputs
    length = 2 * (depth // inputs + 1) * lanes
    return pl.pallas_call(
        functools.partial(visibility_kernel, inputs, scale),
        in_specs=[pl.BlockSpec(memory_space=pltpu.SMEM)]
        + [pl.BlockSpec(memory_space=pltpu.VMEM)] * len(sources),
        out_specs=pl.BlockSpec(memory_space=pl.ANY),
        scratch_shapes=[
            pltpu.VMEM((total, length), BF16),
            pltpu.VMEM((total // 2, length), BF16),
            pltpu.VMEM((total // COLUMNS, 2, total // 2, COLUMNS), F32),
            pltpu.SemaphoreType.DMA((total // COLUMNS, 2)),
        ],
        out_shape=jax.ShapeDtypeStruct((2, 1, total // 2, total), F32),
        compiler_params=pltpu.CompilerParams(vmem_limit_bytes=VMEM_VIS),
        cost_estimate=pl.CostEstimate(
            flops=2 * total * total * length, bytes_accessed=7 * MIB, transcendentals=0
        ),
    )(where, *sources)


def swap(array, far_x, far_t):
    route = [(t * 2 + x, (t ^ far_t) * 2 + (x ^ far_x)) for t in range(2) for x in range(2)]
    return lax.ppermute(array, ("ta", "xh"), route)


def along_x(mine, theirs):
    both = swap(theirs, 1, 1)
    far = swap(theirs, 1, 0)
    near = swap(mine, 0, 1)
    return [mine, far, near, both]


def over_plane(array):
    return lax.all_to_all(array, PLANE, split_axis=0, concat_axis=0, tiled=True)


def by_x(array, axis):
    x_hi = lax.axis_index("xh")
    return [lax.dynamic_index_in_dim(array, at, axis, keepdims=False) for at in (x_hi, 1 - x_hi)]


def local(voltages):
    inputs = voltages.shape[0]
    spectra = voltages.shape[1] // FRAME
    n_time = lax.axis_size("ta")
    n_plane = lax.axis_size(PLANE)
    n_chan = 2 * n_plane
    window = jnp.asarray(pfb_window())
    channels = np.arange(n_chan).reshape(N_Y, 2, -1).swapaxes(0, 1)
    x_first = jnp.asarray(dft_table(channels.reshape(-1)))
    x_last = jnp.asarray(dft_table(channels.reshape(2, -1).T.reshape(-1)))
    frames = voltages.reshape(inputs, spectra, FRAME).transpose(1, 0, 2)
    start = spectra // 4 * (4 - FIRST)

    late, last = filterbank(
        frames, start, spectra - start, frames, start - HALO, window, x_last, True
    )
    turned_late = over_plane(late.reshape(n_plane, 2, *late.shape[1:]))
    earlier = lax.ppermute(last, "ta", [(i, (i + 1) % n_time) for i in range(n_time)])
    earlier = jnp.where(lax.axis_index("ta") == 0, jnp.zeros_like(earlier), earlier)
    (early,) = filterbank(frames, 0, start, earlier, 0, window, x_first, False)
    sources_early = along_x(*by_x(early.reshape(2, n_plane, *early.shape[1:]), 0))
    stacked = jnp.concatenate(sources_early, 1)
    turned_late, stacked = lax.optimization_barrier((turned_late, stacked))
    sources_late = along_x(*by_x(turned_late, 1))
    turned_early = over_plane(stacked)

    where = jnp.stack([lax.axis_index("ta"), lax.axis_index("xh")]).astype(jnp.int32)
    scale = 1.0 / (16.0 * FRAME * spectra * n_time)
    mine, far, near, both = sources_late
    far = as_rows(far, inputs)
    return visibilities(where, [mine, far, near, both, turned_early], inputs, scale)


def solution(mesh):
    fine = Mesh(mesh.devices.reshape(2, 4, 2, 8, 2), ("ta", "y", "xh", "z", "core"))
    gx = ("y", "xh", "z", "core")
    return jax.shard_map(
        local, mesh=fine, in_specs=(P(gx, "ta"),), out_specs=P(None, gx, "ta", None), check_vma=False
    )
```

```python
import functools

import jax
import jax.numpy as jnp
import ml_dtypes
import numpy as np
from jax import lax
from jax.experimental import pallas as pl
from jax.experimental.pallas import tpu as pltpu
from jax.sharding import Mesh
from jax.sharding import PartitionSpec as P

FRAME = 2048
TAPS = 4
UNIT = 64
PIECE = 32
GROUP = 8
HALO = 4
FIRST = 3
DEPTH = 512
N_Y = 4
PLANE = ("y", "z", "core")
BANK_FLOPS = 20 * 1024**3
ROWS_FLOPS = 9 * 1024**3
COLUMNS = 512
MIB = 1024 * 1024
VMEM_BANK = 56 * MIB
VMEM_VIS = 28 * MIB
F32 = jnp.float32
BF16 = jnp.bfloat16


def pfb_window():
    length = TAPS * FRAME
    points = np.arange(length, dtype=np.float64)
    window = np.sinc((points - length / 2 + 0.5) / FRAME) * (
        0.54 - 0.46 * np.cos(2.0 * np.pi * points / (length - 1))
    )
    return window.reshape(TAPS, FRAME).astype(np.float32)


def dft_table(order):
    phase = (np.arange(FRAME)[:, None] * order[None, :] % FRAME) * (2.0 * np.pi / FRAME)
    return np.concatenate([np.cos(phase), -np.sin(phase)], 1).astype(ml_dtypes.bfloat16)


def filterbank_kernel(first, halo_at, frames, halo, window, table, *refs):
    out, (held, weight, dft, summed, turned, ready, sem) = refs[0], refs[-7:]
    inputs = held.shape[1]
    count, depth = ready.shape[:2]
    units = depth // inputs
    span = PIECE * inputs
    pieces = UNIT // PIECE

    def copy(piece):
        return pltpu.make_async_copy(
            frames.at[pl.ds(first + piece * PIECE, PIECE)],
            held.at[pl.ds(HALO + piece * PIECE, PIECE)],
            sem.at[3 + piece],
        )

    halo_copy = pltpu.make_async_copy(
        halo.at[pl.ds(halo_at, HALO)], held.at[pl.ds(0, HALO)], sem.at[0]
    )
    table_copy = pltpu.make_async_copy(table, dft, sem.at[1])
    window_copy = pltpu.make_async_copy(window, weight, sem.at[2])
    window_copy.start()
    halo_copy.start()
    copy(0).start()
    table_copy.start()
    for piece in range(1, units * pieces):
        copy(piece).start()
    window_copy.wait()
    halo_copy.wait()

    table_copy.wait()

    def split(piece, lanes):
        high, rest = [], []
        for g in range(PIECE // GROUP):
            at = piece * PIECE + g * GROUP + HALO - TAPS + 1
            some = held[pl.ds(at, GROUP + TAPS - 1), :, lanes].astype(F32)
            total = weight[0:1, lanes][None] * some[0:GROUP]
            for k in range(1, TAPS):
                total = total + weight[k : k + 1, lanes][None] * some[k : k + GROUP]
            total = total.reshape(GROUP * inputs, DEPTH)
            high.append(total.astype(BF16))
            rest.append((total - high[-1].astype(F32)).astype(BF16))
        return jnp.concatenate(high + rest, 0)

    def turn(u, i):
        both = jnp.concatenate(
            [summed[lax.rem(u, 2), part, pl.ds(i, UNIT, stride=inputs), :] for part in range(2)], 0
        )
        turned[pl.ds(u * inputs + i, count, stride=units * inputs), :] = both.T

    def body(piece, carry):
        copy(piece).wait()
        u, step = piece // pieces, lax.rem(piece, pieces)
        for i in range(inputs // pieces):
            turn(jnp.maximum(u - 1, 0), step * (inputs // pieces) + i)
        product = None
        for n in range(FRAME // DEPTH):
            lanes = slice(n * DEPTH, (n + 1) * DEPTH)
            term = jnp.dot(split(piece, lanes), dft[lanes, :], preferred_element_type=F32)
            product = term if product is None else product + term
        product = product[:span] + product[span:]
        row = pl.multiple_of(step * span, span)
        for part in range(2):
            summed[lax.rem(u, 2), part, pl.ds(row, span), :] = product[
                :, part * count : (part + 1) * count
            ]
        return carry

    lax.fori_loop(0, units * pieces, body, 0)
    for i in range(inputs):
        turn(units - 1, i)
    copies = [
        pltpu.make_async_copy(held.at[pl.ds(units * UNIT, HALO)], last, sem.at[0])
        for last in refs[1:-7]
    ]
    for copy_out in copies:
        copy_out.start()
    share = count // 4
    for quarter in range(4):
        some = turned[quarter * share * units * inputs : (quarter + 1) * share * units * inputs, :]
        here = pl.ds(quarter * share, share)
        ready[here] = some.reshape(share, units * inputs, 2 * UNIT).astype(BF16)
        copies.append(pltpu.make_async_copy(ready.at[here], out.at[here], sem.at[3 + quarter]))
        copies[-1].start()
    for copy_out in copies:
        copy_out.wait()


def filterbank(frames, first, spectra, halo, halo_at, window, table, tail):
    _, inputs, _ = frames.shape
    count = table.shape[1] // 2
    units = spectra // UNIT
    there = pl.BlockSpec(memory_space=pl.ANY)
    return pl.pallas_call(
        functools.partial(filterbank_kernel, first, halo_at),
        in_specs=[there] * 4,
        out_specs=[there] * (1 + tail),
        out_shape=[
            jax.ShapeDtypeStruct((count, units * inputs, 2 * UNIT), BF16),
            jax.ShapeDtypeStruct((HALO, inputs, FRAME), BF16),
        ][: 1 + tail],
        scratch_shapes=[
            pltpu.VMEM((HALO + spectra, inputs, FRAME), BF16),
            pltpu.VMEM(window.shape, F32),
            pltpu.VMEM(table.shape, BF16),
            pltpu.VMEM((2, 2, UNIT * inputs, count), F32),
            pltpu.VMEM((count * units * inputs, 2 * UNIT), F32),
            pltpu.VMEM((count, units * inputs, 2 * UNIT), BF16),
            pltpu.SemaphoreType.DMA((3 + max(4, spectra // PIECE),)),
        ],
        compiler_params=pltpu.CompilerParams(vmem_limit_bytes=VMEM_BANK),
        cost_estimate=pl.CostEstimate(
            flops=BANK_FLOPS,
            bytes_accessed=2 * spectra * inputs * FRAME + MIB,
            transcendentals=0,
        ),
    )(frames, halo, window, table)


def rows_kernel(inputs, source, out):
    groups, depth, _ = source.shape
    units = depth // inputs
    wide = source[...].astype(F32).reshape(groups, units, inputs, 2 * UNIT)
    for u in range(units):
        rows = wide[:, u].reshape(groups * inputs, 2 * UNIT).astype(BF16)
        out[u * groups * inputs : (u + 1) * groups * inputs, :] = rows


def as_rows(source, inputs):
    groups, depth, lanes = source.shape
    here = pl.BlockSpec(memory_space=pltpu.VMEM)
    return pl.pallas_call(
        functools.partial(rows_kernel, inputs),
        in_specs=[here],
        out_specs=here,
        out_shape=jax.ShapeDtypeStruct((groups * depth, lanes), BF16),
        compiler_params=pltpu.CompilerParams(vmem_limit_bytes=VMEM_VIS),
        cost_estimate=pl.CostEstimate(flops=ROWS_FLOPS, bytes_accessed=MIB, transcendentals=0),
    )(source)


def visibility_kernel(inputs, scale, where, mine, far, near, both, small, out, right, left, ready, sem):
    groups = mine.shape[0]
    units = mine.shape[1] // inputs
    n_rows = left.shape[0]
    stripe = groups // N_Y * inputs
    n_lanes = 2 * UNIT

    def place(rows, origin, unit):
        x_hi = (where[1] + origin % 2) % 2
        segment = origin // 2 * (units + 1) + unit
        for y in range(N_Y):
            row = pl.multiple_of((2 * y + x_hi) * stripe, stripe)
            right[pl.ds(row, stripe), segment * n_lanes : (segment + 1) * n_lanes] = rows[
                y * stripe : (y + 1) * stripe
            ]

    for origin, source in ((0, mine), (2, near), (3, both)):
        wide = source[...].astype(F32).reshape(groups, units, inputs, n_lanes)
        for u in range(units):
            place(wide[:, u].reshape(groups * inputs, n_lanes).astype(BF16), origin, u)
    for u in range(units):
        place(far[u * groups * inputs : (u + 1) * groups * inputs, :], 1, u)
    wide = small[...].astype(F32).reshape(groups, 4, inputs, n_lanes)
    for origin in range(4):
        place(wide[:, origin].reshape(groups * inputs, n_lanes).astype(BF16), origin, units)
    own = pl.ds(pl.multiple_of(where[0] * n_rows, n_rows), n_rows)
    lane = lax.broadcasted_iota(jnp.int32, (n_rows, n_lanes), 1)
    copies = []
    for part in range(2):
        if part == 1:
            for s in range(right.shape[1] // n_lanes):
                lanes = slice(s * n_lanes, (s + 1) * n_lanes)
                swapped = pltpu.roll(right[own, lanes].astype(F32), UNIT, 1)
                left[:, lanes] = jnp.where(lane < UNIT, swapped, -swapped).astype(BF16)
        for block in range(right.shape[0] // COLUMNS):
            columns = slice(block * COLUMNS, (block + 1) * COLUMNS)
            product = lax.dot_general(
                left[...] if part else right[own, :],
                right[columns, :],
                (((1,), (1,)), ((), ())),
                preferred_element_type=F32,
            )
            ready[block, part] = product * scale
            copies.append(
                pltpu.make_async_copy(
                    ready.at[block, part], out.at[part, 0, :, columns], sem.at[block, part]
                )
            )
            copies[-1].start()
    for copy in copies:
        copy.wait()


def visibilities(where, sources, inputs, scale):
    groups, depth, lanes = sources[0].shape
    total = 2 * groups * inputs
    length = 2 * (depth // inputs + 1) * lanes
    return pl.pallas_call(
        functools.partial(visibility_kernel, inputs, scale),
        in_specs=[pl.BlockSpec(memory_space=pltpu.SMEM)]
        + [pl.BlockSpec(memory_space=pltpu.VMEM)] * len(sources),
        out_specs=pl.BlockSpec(memory_space=pl.ANY),
        scratch_shapes=[
            pltpu.VMEM((total, length), BF16),
            pltpu.VMEM((total // 2, length), BF16),
            pltpu.VMEM((total // COLUMNS, 2, total // 2, COLUMNS), F32),
            pltpu.SemaphoreType.DMA((total // COLUMNS, 2)),
        ],
        out_shape=jax.ShapeDtypeStruct((2, 1, total // 2, total), F32),
        compiler_params=pltpu.CompilerParams(vmem_limit_bytes=VMEM_VIS),
        cost_estimate=pl.CostEstimate(
            flops=2 * total * total * length, bytes_accessed=7 * MIB, transcendentals=0
        ),
    )(where, *sources)


def swap(array, far_x, far_t):
    route = [(t * 2 + x, (t ^ far_t) * 2 + (x ^ far_x)) for t in range(2) for x in range(2)]
    return lax.ppermute(array, ("ta", "xh"), route)


def along_x(mine, theirs):
    both = swap(theirs, 1, 1)
    far = swap(theirs, 1, 0)
    near = swap(mine, 0, 1)
    return [mine, far, near, both]


def over_plane(array):
    return lax.all_to_all(array, PLANE, split_axis=0, concat_axis=0, tiled=True)


def by_x(array, axis):
    x_hi = lax.axis_index("xh")
    return [lax.dynamic_index_in_dim(array, at, axis, keepdims=False) for at in (x_hi, 1 - x_hi)]


def local(voltages):
    inputs = voltages.shape[0]
    spectra = voltages.shape[1] // FRAME
    n_time = lax.axis_size("ta")
    n_plane = lax.axis_size(PLANE)
    n_chan = 2 * n_plane
    window = jnp.asarray(pfb_window())
    channels = np.arange(n_chan).reshape(N_Y, 2, -1).swapaxes(0, 1)
    x_first = jnp.asarray(dft_table(channels.reshape(-1)))
    x_last = jnp.asarray(dft_table(channels.reshape(2, -1).T.reshape(-1)))
    frames = voltages.reshape(inputs, spectra, FRAME).transpose(1, 0, 2)
    start = spectra // 4 * (4 - FIRST)

    late, last = filterbank(
        frames, start, spectra - start, frames, start - HALO, window, x_last, True
    )
    turned_late = over_plane(late.reshape(n_plane, 2, *late.shape[1:]))
    earlier = lax.ppermute(last, "ta", [(i, (i + 1) % n_time) for i in range(n_time)])
    earlier = jnp.where(lax.axis_index("ta") == 0, jnp.zeros_like(earlier), earlier)
    (early,) = filterbank(frames, 0, start, earlier, 0, window, x_first, False)
    sources_early = along_x(*by_x(early.reshape(2, n_plane, *early.shape[1:]), 0))
    stacked = jnp.concatenate(sources_early, 1)
    turned_late, stacked = lax.optimization_barrier((turned_late, stacked))
    sources_late = along_x(*by_x(turned_late, 1))
    turned_early = over_plane(stacked)

    where = jnp.stack([lax.axis_index("ta"), lax.axis_index("xh")]).astype(jnp.int32)
    scale = 1.0 / (16.0 * FRAME * spectra * n_time)
    mine, far, near, both = sources_late
    far = as_rows(far, inputs)
    return visibilities(where, [mine, far, near, both, turned_early], inputs, scale)


def solution(mesh):
    fine = Mesh(mesh.devices.reshape(2, 4, 2, 8, 2), ("ta", "y", "xh", "z", "core"))
    gx = ("y", "xh", "z", "core")
    return jax.shard_map(
        local, mesh=fine, in_specs=(P(gx, "ta"),), out_specs=P(None, gx, "ta", None), check_vma=False
    )
```
